32 devices in a mesh: groups: 2 (over y), vocab: 8 (over z, x), tok: 2 (over core).
Axes of the slice: x: 2, y: 2, z: 4, core: 2. Of those that a mesh axis runs over, the one named last changes fastest.
Arguments:
- hidden_rows: bfloat16 [512, 4096], P(('groups', 'vocab'), 'tok'), parts along dimension 0, may hold values from -4 to 4
- head_weight: bfloat16 [4096, 6144], P('tok', 'vocab'), may hold values from -4 to 4
- block_links: int32 [2, 64], P(None, 'vocab'), may hold values from -1 to 2, as said below
- teacher_rows: int32 [64, 128], P('vocab'), may hold values from 0 to 255, as said below
- offsets: int32 [64, 4, 128], P('vocab'), may hold values from 0 to 255, as said below
- link_weights: bfloat16 [64, 4, 128], P('vocab'), may hold values from 0.049804688 to 1
Outputs:
- log_partition: float32 [512], P(('groups', 'tok')), parts along dimension 0
- student_targets: float32 [512, 6144], P(('groups', 'tok'), 'vocab'), parts along dimension 0
The draws below stay inside these ranges and needn't reach their ends.
There are 2 independent parts, one for each index of `groups`. The reference program is written for one: setup_inputs(seed, part) draws one part's arguments, and reference() takes and returns one part's arrays. A program takes and returns all parts, laid end to end along the dimension named above; an argument that names none is the same for every part. Nothing has to cross between parts.
Inputs may be any that keep to these rules, and one draw needn't show every extreme that they name: `block_links`: row 0 of a slot is a teacher block of its shard, 0 to 2; row 1 is a block of the owner's 3 student blocks, or -1 where the slot is padding. Every teacher block of every shard has a live slot. `teacher_rows`: the 128 entries of one slot are distinct entries of its teacher block; every teacher entry of every shard is used by some live slot. The 4 offsets of one used teacher entry of a slot are distinct.
All inputs are finite; a program needn't handle non-finite values.
Results may differ from the reference program's by a relative error of at most 0.0029.
Values may be sent and summed in bfloat16 or wider, within the bound.
A program may use at most 64 MiB of HBM per device.

```python
import math
import jax
import jax.numpy as jnp
from jax import lax

D = 4096
BLOCK = 256
K = 4
USED = 128
TB_DEV = 3
SB_DEV = 3
TOKENS = 256
VT = 6144
VS = 6144
N_VOCAB = 8


def draw_hidden_rows(key, part):
    key = jax.random.fold_in(key, 11)
    first_key, second_key = jax.random.split(key)
    scales = jnp.exp(jax.random.uniform(second_key, (TOKENS, 1), jnp.float32, math.log(0.5), math.log(1.0)))
    raw_values = jnp.clip(jax.random.normal(first_key, (TOKENS, D), jnp.float32), -4.0, 4.0)
    return (raw_values * scales).astype(jnp.bfloat16)


def draw_head_weight(key, part):
    key = jax.random.fold_in(key, 23)
    first_key, second_key = jax.random.split(key, 2)
    raw_values = jnp.clip(jax.random.normal(first_key, (D, VT), jnp.float32), -5.0, 5.0)
    column_scale = jnp.exp(jax.random.uniform(second_key, (1, VT), jnp.float32, math.log(0.5), math.log(1.5)))
    return (raw_values * column_scale / math.sqrt(D)).astype(jnp.bfloat16)


def draw_block_links(key, part):
    key = jax.random.fold_in(key, 37)
    first_key, second_key, third_key = jax.random.split(key, 3)
    slot_total = N_VOCAB * N_VOCAB
    slot_index = jnp.arange(slot_total, dtype=jnp.int32)
    source = slot_index // N_VOCAB
    owner = slot_index % N_VOCAB
    distance = (owner - source) % N_VOCAB
    forced = distance < 2 * TB_DEV
    teacher = jnp.where(forced, distance % TB_DEV, jax.random.randint(first_key, (slot_total,), 0, TB_DEV))
    live = forced | (jax.random.randint(second_key, (slot_total,), 0, 4) != 0)
    student = jnp.where(live, jax.random.randint(third_key, (slot_total,), 0, SB_DEV), -1)
    return jnp.stack([teacher, student]).astype(jnp.int32)


def draw_teacher_rows(key, part):
    key = jax.random.fold_in(key, 53)
    first_key, second_key = jax.random.split(key)
    slot_total = N_VOCAB * N_VOCAB
    slot_index = jnp.arange(slot_total, dtype=jnp.int32)
    source = slot_index // N_VOCAB
    distance = (slot_index % N_VOCAB - source) % N_VOCAB
    iota_row = jnp.arange(BLOCK, dtype=jnp.int32)[None, :]
    shared_scores = jax.random.randint(first_key, (N_VOCAB * TB_DEV, BLOCK), 0, 1 << 20) * BLOCK + iota_row
    shared_order = jnp.argsort(shared_scores, axis=1).astype(jnp.int32)
    own_scores = jax.random.randint(second_key, (slot_total, BLOCK), 0, 1 << 20) * BLOCK + iota_row
    own_order = jnp.argsort(own_scores, axis=1).astype(jnp.int32)
    forced_block = source * TB_DEV + distance % TB_DEV
    from_shared = jnp.take(shared_order, forced_block, axis=0)
    lower = from_shared[:, :USED]
    upper = from_shared[:, USED:]
    chosen = jnp.where((distance < TB_DEV)[:, None], lower, jnp.where((distance < 2 * TB_DEV)[:, None], upper, own_order[:, :USED]))
    return chosen.astype(jnp.int32)


def draw_offsets(key, part):
    key = jax.random.fold_in(key, 41)
    first_key, second_key = jax.random.split(key)
    slot_total = N_VOCAB * N_VOCAB
    quarter = BLOCK // K
    base = jax.random.randint(first_key, (slot_total, 1, USED), 0, BLOCK)
    jitter = jax.random.randint(second_key, (slot_total, K, USED), 0, quarter)
    lanes = jnp.arange(K, dtype=jnp.int32).reshape(1, K, 1) * quarter
    return ((base + lanes + jitter) % BLOCK).astype(jnp.int32)


def level_of(rng, dims, cuts, least, largest):
    loudness = 1.0
    for axis_at, parts in cuts:
        steps = jax.random.uniform(jax.random.fold_in(jax.random.fold_in(rng, 6), axis_at), (parts,), jnp.float32, least / len(cuts), largest / len(cuts))
        loudness = loudness * jnp.repeat(jnp.exp(steps), dims[axis_at] // parts).reshape((-1,) + (1,) * (len(dims) - 1 - axis_at))
    return loudness


def setup_inputs(seed: int = 0, part: int = 0) -> dict:
    key_list = jax.random.split(jax.random.key(seed), 7)
    own_keys = jax.random.split(jax.random.fold_in(key_list[6], part), 7)
    return {
        "hidden_rows": draw_hidden_rows(jax.random.fold_in(jax.random.fold_in(key_list[6], part), 71), part),
        "head_weight": draw_head_weight(jax.random.fold_in(key_list[6], 71), part),
        "block_links": draw_block_links(jax.random.fold_in(key_list[6], 71), part),
        "teacher_rows": draw_teacher_rows(jax.random.fold_in(key_list[6], 71), part),
        "offsets": draw_offsets(jax.random.fold_in(key_list[6], 71), part),
        "link_weights": jnp.clip(jnp.exp(math.log(1.0) - 2.9996462 * jax.random.uniform(key_list[5], (N_VOCAB * N_VOCAB, K, USED), jnp.float32) ** level_of(key_list[5], (N_VOCAB * N_VOCAB, K, USED), ((0, 8),), -0.2, 0.2)), 0.049804688, 1.0).astype(jnp.bfloat16),
    }


def dense_blocks(columns, weights, width):
    positions = lax.broadcasted_iota(jnp.int32, (1, 1, width), 2)
    dense_block = jnp.zeros((columns.shape[0], columns.shape[2], width), jnp.bfloat16)
    for member in range(columns.shape[1]):
        dense_block = jnp.where(columns[:, member, :, None] == positions, weights[:, member, :, None], dense_block)
    return dense_block


def reference(hidden_rows, head_weight, block_links, teacher_rows, offsets, link_weights):
    logits = jnp.dot(hidden_rows, head_weight, preferred_element_type=jnp.float32)
    row_peak = jnp.max(logits, axis=1)
    exponent = jnp.exp(logits - row_peak[:, None])
    row_mass = jnp.sum(exponent, axis=1)
    log_partition = row_peak + jnp.log(row_mass)
    teacher_probs = (exponent / row_mass[:, None]).astype(jnp.bfloat16)
    token_count = teacher_probs.shape[0]
    by_shard = teacher_probs.reshape(token_count, N_VOCAB, TB_DEV * BLOCK).transpose(1, 2, 0)
    links_by_shard = block_links.reshape(2, N_VOCAB, N_VOCAB).transpose(1, 0, 2)
    rows_by_shard = teacher_rows.reshape(N_VOCAB, N_VOCAB, USED)
    offsets_by_shard = offsets.reshape(N_VOCAB, N_VOCAB, K, USED)
    weights_by_shard = link_weights.reshape(N_VOCAB, N_VOCAB, K, USED)
    owner_base = jnp.arange(N_VOCAB, dtype=jnp.int32) * SB_DEV

    def one_shard(aligned, inputs):
        shard_probs, links, used_rows, columns, weights = inputs
        wanted = (links[0][:, None] * BLOCK + used_rows).astype(jnp.int32)
        picked = jnp.take(shard_probs, wanted, axis=0)
        dense_block = dense_blocks(columns, weights, BLOCK)
        pieces = jnp.einsum("ncr,ncd->nrd", picked.astype(jnp.float32), dense_block.astype(jnp.float32))
        pieces = lax.optimization_barrier(pieces.astype(jnp.bfloat16)).astype(jnp.float32)
        live = links[1] >= 0
        pieces = jnp.where(live[:, None, None], pieces, jnp.float32(0.0))
        target = (owner_base + jnp.maximum(links[1], 0)).astype(jnp.int32)
        return aligned.at[target].add(pieces), None

    start_value = jnp.zeros((N_VOCAB * SB_DEV, token_count, BLOCK), jnp.float32)
    aligned, unused = lax.scan(one_shard, start_value, (by_shard, links_by_shard, rows_by_shard, offsets_by_shard, weights_by_shard))
    row_total = jnp.sum(aligned, axis=(0, 2))
    student = aligned.transpose(1, 0, 2).reshape(token_count, VS)
    return log_partition, VS * student / row_total[:, None]
```

```python
import functools
import math

import jax
import jax.numpy as jnp
from jax import lax
from jax.experimental import pallas as pl
from jax.experimental.pallas import tpu as pltpu
from jax.sharding import PartitionSpec as P

BLOCK = 256
SB_DEV = 3


def combined_all(value, axis, join):
    pieces = jax.tree.map(lambda part: lax.all_gather(part, axis), value)
    head = jax.tree.map(lambda part: part[0], pieces)
    tail = jax.tree.map(lambda part: part[1:], pieces)
    so_far, _ = lax.scan(lambda so_far, share: (join(so_far, share), None), head, tail)
    return so_far


def dense_blocks(columns, weights, width):
    positions = lax.broadcasted_iota(jnp.int32, (1, 1, width), 2)
    dense_block = jnp.zeros((columns.shape[0], columns.shape[2], width), jnp.bfloat16)
    for member in range(columns.shape[1]):
        dense_block = jnp.where(
            columns[:, member, :, None] == positions, weights[:, member, :, None], dense_block
        )
    return dense_block


def aligned_pieces(picked, columns, weights):
    slot_count = picked.shape[0]
    group_size = math.gcd(slot_count, 16)
    group_count = slot_count // group_size

    def one_group(inputs):
        chosen_in, columns_in, weights_in = inputs
        dense_block = dense_blocks(columns_in, weights_in, BLOCK)
        product = jnp.einsum(
            "gcr,gcd->grd", chosen_in, dense_block, preferred_element_type=jnp.float32
        )
        return product.astype(jnp.bfloat16)

    shaped = (
        picked.reshape((group_count, group_size) + picked.shape[1:]),
        columns.reshape((group_count, group_size) + columns.shape[1:]),
        weights.reshape((group_count, group_size) + weights.shape[1:]),
    )
    return lax.map(one_group, shaped).reshape(slot_count, picked.shape[2], BLOCK)


def collect(received, arrived, blocks_here):
    wanted = lax.broadcasted_iota(jnp.int32, (arrived.shape[0], blocks_here), 1)
    selector = (arrived[:, None] == wanted).astype(jnp.bfloat16)
    summed = jnp.einsum("srd,sj->rjd", received, selector, preferred_element_type=jnp.float32)
    return summed.reshape(received.shape[1], blocks_here * received.shape[2])


def local(hidden_rows, head_weight, block_links, teacher_rows, offsets, link_weights):
    halves = jnp.dot(
        lax.all_gather(hidden_rows, "vocab", axis=0, tiled=True),
        head_weight,
        preferred_element_type=jnp.float32,
    )
    logits = lax.psum_scatter(halves, "tok", scatter_dimension=0, tiled=True)
    local_peak = jnp.max(logits, axis=1)
    local_mass = jnp.sum(jnp.exp(logits - local_peak[:, None]), axis=1)

    def combine(earlier, later):
        top_value = jnp.maximum(earlier[0], later[0])
        joined = earlier[1] * jnp.exp(earlier[0] - top_value) + later[1] * jnp.exp(
            later[0] - top_value
        )
        return (top_value, joined)

    row_peak, row_mass = combined_all((local_peak, local_mass), "vocab", combine)
    exponent = jnp.exp(logits - row_peak[:, None])
    teacher_probs = (exponent / row_mass[:, None]).astype(jnp.bfloat16)
    by_column = teacher_probs.T
    columns_wanted = block_links[0][:, None] * BLOCK + teacher_rows
    picked = jnp.take(by_column, columns_wanted, axis=0)
    targets = block_links[1][:, None]
    pieces = aligned_pieces(picked, offsets, link_weights)
    received, arrived = (
        lax.all_to_all(pieces, "vocab", split_axis=0, concat_axis=0, tiled=True),
        lax.all_to_all(targets, "vocab", split_axis=0, concat_axis=0, tiled=True),
    )
    aligned = collect(received, arrived[:, 0], SB_DEV)
    row_total = lax.psum(jnp.sum(aligned, axis=1), "vocab")
    student_width = aligned.shape[1] * lax.axis_size("vocab")
    student_targets = student_width * aligned / row_total[:, None]
    return (row_peak + jnp.log(row_mass), student_targets)


MESH = pl.DeviceIdType.MESH


def fused_kernel(
    n,
    hidden_ref,
    weight_ref,
    links_ref,
    rows_ref,
    offsets_ref,
    link_weights_ref,
    log_ref,
    target_ref,
    held,
    weight,
    own_half,
    other_half,
    arrived_half,
    exponents,
    onehot,
    meta_out,
    meta_in,
    dense,
    used_out,
    used_in,
    stats_out,
    stats_in,
    local_sems,
    hidden_send,
    hidden_recv,
    meta_send,
    meta_recv,
    half_send,
    half_recv,
    used_send,
    used_recv,
    stats_send,
    stats_recv,
):
    group, me, tok = lax.axis_index("groups"), lax.axis_index("vocab"), lax.axis_index("tok")
    columns = weight.shape[1]
    tiles = columns // BLOCK
    half_blocks = n // 2
    tokens = own_half.shape[0]
    used = rows_ref.shape[1]

    def peer(index):
        return (group, index, tok)

    sibling = (group, me, 1 - tok)

    def remote(source, target, send, recv, device):
        return pltpu.make_async_remote_copy(
            src_ref=source,
            dst_ref=target,
            send_sem=send,
            recv_sem=recv,
            device_id=device,
            device_id_type=MESH,
        )

    def others():
        return [lax.rem(me + step, n) for step in range(1, n)]

    barrier = pltpu.get_barrier_semaphore()
    for other in others():
        pl.semaphore_signal(barrier, inc=1, device_id=peer(other), device_id_type=MESH)
    pl.semaphore_signal(barrier, inc=1, device_id=sibling, device_id_type=MESH)
    weight_copy = pltpu.make_async_copy(weight_ref, weight, local_sems.at[0])
    weight_copy.start()
    own_copy = pltpu.make_async_copy(hidden_ref, held.at[me], local_sems.at[1])
    own_copy.start()
    values = link_weights_ref[...].astype(jnp.float32)
    for slot in range(n):
        place = offsets_ref[slot] + links_ref[1, slot] * BLOCK
        meta_out[slot, 0:4, :] = place.astype(jnp.float32)
        meta_out[slot, 4:8, :] = values[slot]
    pl.semaphore_wait(barrier, n)

    across = me + 1 - 2 * lax.rem(me, 2)
    line = [lax.rem(me + 2 * step, n) for step in range(1, n // 2)]
    sends = []

    def launch(copy):
        copy.start()
        sends.append(copy)

    launch(remote(hidden_ref, held.at[me], hidden_send.at[0], hidden_recv.at[me], peer(across)))
    for step, other in enumerate(line):
        launch(
            remote(
                hidden_ref,
                held.at[me],
                hidden_send.at[1 + step],
                hidden_recv.at[me],
                peer(other),
            )
        )
    for step, other in enumerate(others()):
        launch(
            remote(
                meta_out.at[other],
                meta_in.at[me],
                meta_send.at[step],
                meta_recv.at[me],
                peer(other),
            )
        )
    meta_in[me] = meta_out[me]

    row_index = lax.broadcasted_iota(jnp.int32, (BLOCK, used), 0)
    for slot in range(n):
        onehot[slot] = (rows_ref[slot : slot + 1, :] == row_index).astype(jnp.bfloat16)

    def wait_hidden(source):
        remote(
            held.at[source], held.at[source], hidden_send.at[0], hidden_recv.at[source], sibling
        ).wait_recv()

    for step, other in enumerate(line):
        wait_hidden(other)
        launch(
            remote(
                held.at[other],
                held.at[other],
                hidden_send.at[n // 2 + step],
                hidden_recv.at[other],
                peer(across),
            )
        )

    place_index = lax.broadcasted_iota(jnp.int32, (BLOCK, used), 0).astype(jnp.float32)

    def build_dense(source):
        meta = meta_in[source]
        for tile in range(tiles):
            block = jnp.zeros((BLOCK, used), jnp.float32)
            for member in range(4):
                place = meta[member : member + 1, :] - float(tile * BLOCK)
                block = jnp.where(place == place_index, meta[4 + member : 5 + member, :], block)
            dense[source, tile * BLOCK : (tile + 1) * BLOCK, :] = block.astype(jnp.bfloat16)

    for other in others():
        remote(
            meta_in.at[other], meta_in.at[other], meta_send.at[0], meta_recv.at[other], sibling
        ).wait_recv()
        build_dense(other)
    build_dense(me)

    weight_copy.wait()
    own_copy.wait()
    wait_hidden(across)
    for other in line:
        wait_hidden(other + across - me)

    def half_rows(which):
        blocks = held[pl.ds(which * half_blocks, half_blocks)]
        return blocks.reshape(tokens, blocks.shape[2])

    for tile in range(tiles):
        cut = slice(tile * BLOCK, (tile + 1) * BLOCK)
        other_half[tile] = jnp.dot(
            half_rows(1 - tok), weight[:, cut], preferred_element_type=jnp.float32
        )
        launch(
            remote(
                other_half.at[tile],
                arrived_half.at[tile],
                half_send.at[tile],
                half_recv.at[tile],
                sibling,
            )
        )
    for tile in range(tiles):
        cut = slice(tile * BLOCK, (tile + 1) * BLOCK)
        own_half[:, cut] = jnp.dot(
            half_rows(tok), weight[:, cut], preferred_element_type=jnp.float32
        )
    for tile in range(tiles):
        cut = slice(tile * BLOCK, (tile + 1) * BLOCK)
        remote(
            other_half.at[tile],
            arrived_half.at[tile],
            half_send.at[tile],
            half_recv.at[tile],
            sibling,
        ).wait_recv()
        own_half[:, cut] = own_half[:, cut] + arrived_half[tile]

    logits = own_half[...]
    peak = jnp.max(logits, axis=1, keepdims=True)
    exponent = jnp.exp(logits - peak)
    mass = jnp.sum(exponent, axis=1, keepdims=True)
    for tile in range(tiles):
        exponents[tile] = exponent[:, tile * BLOCK : (tile + 1) * BLOCK].astype(jnp.bfloat16)

    running = jnp.zeros((tokens, used), jnp.float32)
    for step, other in enumerate(others() + [me]):
        picked = jnp.dot(
            exponents[links_ref[0, other]], onehot[other], preferred_element_type=jnp.float32
        )
        meta = meta_out[other]
        gain = jnp.sum(
            jnp.where(meta[0:4] >= 0.0, meta[4:8], 0.0), axis=0, keepdims=True
        )
        running = running + picked * gain
        if step < n - 1:
            used_out[step] = picked.astype(jnp.bfloat16)
            launch(
                remote(
                    used_out.at[step],
                    used_in.at[me],
                    used_send.at[step],
                    used_recv.at[me],
                    peer(other),
                )
            )
        else:
            used_in[me] = picked.astype(jnp.bfloat16)
    total = jnp.sum(running, axis=1, keepdims=True)

    lane = lax.broadcasted_iota(jnp.int32, (tokens, 128), 1)
    packed = jnp.where(lane == 0, peak, jnp.where(lane == 1, mass, total))
    stats_out[...] = packed.T[0:8, :]
    for step, other in enumerate(others()):
        launch(
            remote(
                stats_out,
                stats_in.at[me],
                stats_send.at[step],
                stats_recv.at[me],
                peer(other),
            )
        )
    stats_in[me] = stats_out[...]

    for other in others():
        remote(
            stats_out, stats_in.at[other], stats_send.at[0], stats_recv.at[other], sibling
        ).wait_recv()

    peaks = jnp.concatenate([stats_in[v, 0:1, :] for v in range(n)], axis=0)
    masses = jnp.concatenate([stats_in[v, 1:2, :] for v in range(n)], axis=0)
    totals = jnp.concatenate([stats_in[v, 2:3, :] for v in range(n)], axis=0)
    row_peak = jnp.max(peaks, axis=0, keepdims=True)
    shrink = jnp.exp(peaks - row_peak)
    row_mass = jnp.sum(shrink * masses, axis=0, keepdims=True)
    log_ref[...] = row_peak + jnp.log(row_mass)
    share = shrink / row_mass
    row_total = jnp.sum(share * totals, axis=0, keepdims=True)
    factor = float(columns * n) * share / row_total
    factors = jnp.concatenate([factor, jnp.zeros((128 - n, tokens), jnp.float32)], axis=0).T

    for other in others():
        remote(
            used_in.at[other], used_in.at[other], used_send.at[0], used_recv.at[other], sibling
        ).wait_recv()
    for tile in range(tiles):
        cut = slice(tile * BLOCK, (tile + 1) * BLOCK)
        block = jnp.zeros((tokens, BLOCK), jnp.float32)
        for v in range(n):
            piece = lax.dot_general(
                used_in[v],
                dense[v, cut, :],
                (((1,), (1,)), ((), ())),
                preferred_element_type=jnp.float32,
            )
            block = block + factors[:, v : v + 1] * piece
        target_ref[:, cut] = block

    for copy in sends:
        copy.wait_send()


def fused(hidden_rows, head_weight, block_links, teacher_rows, offsets, link_weights):
    n = lax.axis_size("vocab")
    rows, depth = hidden_rows.shape
    columns = head_weight.shape[1]
    tiles = columns // BLOCK
    tokens = rows * n // 2
    used = teacher_rows.shape[1]
    dma = pltpu.SemaphoreType.DMA
    vmem = pl.BlockSpec(memory_space=pltpu.VMEM)
    log_partition, student_targets = pl.pallas_call(
        functools.partial(fused_kernel, n),
        out_shape=(
            jax.ShapeDtypeStruct((1, tokens), jnp.float32),
            jax.ShapeDtypeStruct((tokens, columns), jnp.float32),
        ),
        in_specs=[
            pl.BlockSpec(memory_space=pl.ANY),
            pl.BlockSpec(memory_space=pl.ANY),
            pl.BlockSpec(memory_space=pltpu.SMEM),
            vmem,
            vmem,
            vmem,
        ],
        out_specs=(vmem, vmem),
        scratch_shapes=[
            pltpu.VMEM((n, rows, depth), jnp.bfloat16),
            pltpu.VMEM((depth, columns), jnp.bfloat16),
            pltpu.VMEM((tokens, columns), jnp.float32),
            pltpu.VMEM((tiles, tokens, BLOCK), jnp.float32),
            pltpu.VMEM((tiles, tokens, BLOCK), jnp.float32),
            pltpu.VMEM((tiles, tokens, BLOCK), jnp.bfloat16),
            pltpu.VMEM((n, BLOCK, used), jnp.bfloat16),
            pltpu.VMEM((n, 8, used), jnp.float32),
            pltpu.VMEM((n, 8, used), jnp.float32),
            pltpu.VMEM((n, columns, used), jnp.bfloat16),
            pltpu.VMEM((n - 1, tokens, used), jnp.bfloat16),
            pltpu.VMEM((n, tokens, used), jnp.bfloat16),
            pltpu.VMEM((8, tokens), jnp.float32),
            pltpu.VMEM((n, 8, tokens), jnp.float32),
            dma((2,)),
            dma((n - 1,)),
            dma((n,)),
            dma((n - 1,)),
            dma((n,)),
            dma((tiles,)),
            dma((tiles,)),
            dma((n - 1,)),
            dma((n,)),
            dma((n - 1,)),
            dma((n,)),
        ],
        compiler_params=pltpu.CompilerParams(
            collective_id=0, has_side_effects=True, vmem_limit_bytes=32 * 1024 * 1024
        ),
    )(hidden_rows, head_weight, block_links, teacher_rows, offsets, link_weights)
    return log_partition.reshape(tokens), student_targets


def head(hidden_rows, head_weight, block_links, teacher_rows, offsets, link_weights):
    n = lax.axis_size("vocab")
    rows = hidden_rows.shape[0]
    fits = rows % 16 == 0 and rows * n == 256 and n % 2 == 0 and teacher_rows.shape[0] == n
    form = fused if fits and lax.axis_size("tok") == 2 and n <= 16 else local
    return form(hidden_rows, head_weight, block_links, teacher_rows, offsets, link_weights)


def solution(mesh):
    placed = (
        P(("groups", "vocab"), "tok"),
        P("tok", "vocab"),
        P(None, "vocab"),
        P("vocab", None),
        P("vocab", None, None),
        P("vocab", None, None),
    )
    return jax.shard_map(
        head,
        mesh=mesh,
        in_specs=placed,
        out_specs=(P(("groups", "tok")), P(("groups", "tok"), "vocab")),
        check_vma=False,
    )
```

```python
import functools
import math

import jax
import jax.numpy as jnp
from jax import lax
from jax.experimental import pallas as pl
from jax.experimental.pallas import tpu as pltpu
from jax.sharding import PartitionSpec as P

BLOCK = 256
CHUNKS = 2
SB_DEV = 3


def combined_all(value, axis, join):
    pieces = jax.tree.map(lambda part: lax.all_gather(part, axis), value)
    head = jax.tree.map(lambda part: part[0], pieces)
    tail = jax.tree.map(lambda part: part[1:], pieces)
    so_far, _ = lax.scan(lambda so_far, share: (join(so_far, share), None), head, tail)
    return so_far


def dense_blocks(columns, weights, width):
    positions = lax.broadcasted_iota(jnp.int32, (1, 1, width), 2)
    dense_block = jnp.zeros((columns.shape[0], columns.shape[2], width), jnp.bfloat16)
    for member in range(columns.shape[1]):
        dense_block = jnp.where(
            columns[:, member, :, None] == positions, weights[:, member, :, None], dense_block
        )
    return dense_block


def aligned_pieces(picked, columns, weights):
    slot_count = picked.shape[0]
    group_size = math.gcd(slot_count, 16)
    group_count = slot_count // group_size

    def one_group(inputs):
        chosen_in, columns_in, weights_in = inputs
        dense_block = dense_blocks(columns_in, weights_in, BLOCK)
        product = jnp.einsum(
            "gcr,gcd->grd", chosen_in, dense_block, preferred_element_type=jnp.float32
        )
        return product.astype(jnp.bfloat16)

    shaped = (
        picked.reshape((group_count, group_size) + picked.shape[1:]),
        columns.reshape((group_count, group_size) + columns.shape[1:]),
        weights.reshape((group_count, group_size) + weights.shape[1:]),
    )
    return lax.map(one_group, shaped).reshape(slot_count, picked.shape[2], BLOCK)


def collect(received, arrived, blocks_here):
    wanted = lax.broadcasted_iota(jnp.int32, (arrived.shape[0], blocks_here), 1)
    selector = (arrived[:, None] == wanted).astype(jnp.bfloat16)
    summed = jnp.einsum("srd,sj->rjd", received, selector, preferred_element_type=jnp.float32)
    return summed.reshape(received.shape[1], blocks_here * received.shape[2])


def local(hidden_rows, head_weight, block_links, teacher_rows, offsets, link_weights):
    halves = jnp.dot(
        lax.all_gather(hidden_rows, "vocab", axis=0, tiled=True),
        head_weight,
        preferred_element_type=jnp.float32,
    )
    logits = lax.psum_scatter(halves, "tok", scatter_dimension=0, tiled=True)
    local_peak = jnp.max(logits, axis=1)
    local_mass = jnp.sum(jnp.exp(logits - local_peak[:, None]), axis=1)

    def combine(earlier, later):
        top_value = jnp.maximum(earlier[0], later[0])
        joined = earlier[1] * jnp.exp(earlier[0] - top_value) + later[1] * jnp.exp(
            later[0] - top_value
        )
        return (top_value, joined)

    row_peak, row_mass = combined_all((local_peak, local_mass), "vocab", combine)
    exponent = jnp.exp(logits - row_peak[:, None])
    teacher_probs = (exponent / row_mass[:, None]).astype(jnp.bfloat16)
    by_column = teacher_probs.T
    columns_wanted = block_links[0][:, None] * BLOCK + teacher_rows
    picked = jnp.take(by_column, columns_wanted, axis=0)
    targets = block_links[1][:, None]
    pieces = aligned_pieces(picked, offsets, link_weights)
    received, arrived = (
        lax.all_to_all(pieces, "vocab", split_axis=0, concat_axis=0, tiled=True),
        lax.all_to_all(targets, "vocab", split_axis=0, concat_axis=0, tiled=True),
    )
    aligned = collect(received, arrived[:, 0], SB_DEV)
    row_total = lax.psum(jnp.sum(aligned, axis=1), "vocab")
    student_width = aligned.shape[1] * lax.axis_size("vocab")
    student_targets = student_width * aligned / row_total[:, None]
    return (row_peak + jnp.log(row_mass), student_targets)


MESH = pl.DeviceIdType.MESH


def fused_kernel(
    n,
    hidden_ref,
    weight_ref,
    links_hbm,
    rows_hbm,
    offsets_hbm,
    link_weights_hbm,
    log_ref,
    target_ref,
    links_ref,
    rows_ref,
    offsets_ref,
    link_weights_ref,
    held,
    weight,
    own_half,
    other_half,
    arrived_half,
    exponents,
    onehot,
    meta_out,
    meta_in,
    dense,
    used_out,
    used_in,
    stats_out,
    stats_in,
    local_sems,
    hidden_send,
    hidden_recv,
    meta_send,
    meta_recv,
    half_send,
    half_recv,
    used_send,
    used_recv,
    stats_send,
    stats_recv,
):
    group, me, tok = lax.axis_index("groups"), lax.axis_index("vocab"), lax.axis_index("tok")
    columns = weight.shape[1]
    tiles = columns // BLOCK
    half_blocks = n // 2
    tokens = own_half.shape[0]
    used = rows_ref.shape[1]

    def peer(index):
        return (group, index, tok)

    sibling = (group, me, 1 - tok)

    def remote(source, target, send, recv, device):
        return pltpu.make_async_remote_copy(
            src_ref=source,
            dst_ref=target,
            send_sem=send,
            recv_sem=recv,
            device_id=device,
            device_id_type=MESH,
        )

    def others():
        return [lax.rem(me + step, n) for step in range(1, n)]

    across = me + 1 - 2 * lax.rem(me, 2)
    place_z, last_z = me // 2, n // 2 - 1
    has_lower, has_upper = place_z > 0, place_z < last_z

    barrier = pltpu.get_barrier_semaphore()
    for other in (peer(across), sibling):
        pl.semaphore_signal(barrier, inc=1, device_id=other, device_id_type=MESH)

    @pl.when(has_lower)
    def greet_lower():
        pl.semaphore_signal(barrier, inc=1, device_id=peer(me - 2), device_id_type=MESH)

    @pl.when(has_upper)
    def greet_upper():
        pl.semaphore_signal(barrier, inc=1, device_id=peer(me + 2), device_id_type=MESH)

    weight_copy = pltpu.make_async_copy(weight_ref, weight, local_sems.at[0])
    weight_copy.start()
    own_copy = pltpu.make_async_copy(hidden_ref, held.at[me], local_sems.at[1])
    own_copy.start()
    small_copies = [
        pltpu.make_async_copy(source, target, local_sems.at[2 + index])
        for index, (source, target) in enumerate(
            (
                (links_hbm, links_ref),
                (rows_hbm, rows_ref),
                (offsets_hbm, offsets_ref),
                (link_weights_hbm, link_weights_ref),
            )
        )
    ]
    for copy in small_copies:
        copy.start()
    pl.semaphore_wait(barrier, 2 + (has_lower).astype(jnp.int32) + (has_upper).astype(jnp.int32))

    sends = []

    def launch(copy, live=None):
        sends.append((copy, live))
        if live is None:
            copy.start()
        else:
            pl.when(live)(copy.start)

    part = held.shape[1] // CHUNKS

    def held_part(source, chunk):
        return held.at[source, pl.ds(chunk * part, part)]

    def hidden_copy(source, chunk, send, target, own=False):
        here = hidden_ref.at[pl.ds(chunk * part, part)] if own else held_part(source, chunk)
        return remote(
            here,
            held_part(source, chunk),
            hidden_send.at[send * CHUNKS + chunk],
            hidden_recv.at[source * CHUNKS + chunk],
            peer(target),
        )

    for chunk in range(CHUNKS):
        launch(hidden_copy(me, chunk, 1, me - 2, True), has_lower)
        launch(hidden_copy(me, chunk, 2, me + 2, True), has_upper)
        launch(hidden_copy(me, chunk, 0, across, True))

    for copy in small_copies:
        copy.wait()
    values = link_weights_ref[...].astype(jnp.float32)
    for slot in range(n):
        place = offsets_ref[slot] + links_ref[1, slot] * BLOCK
        meta_out[slot, 0:4, :] = place.astype(jnp.float32)
        meta_out[slot, 4:8, :] = values[slot]
    meta_in[me] = meta_out[me]

    row_index = lax.broadcasted_iota(jnp.int32, (BLOCK, used), 0)
    for slot in range(n):
        onehot[slot] = (rows_ref[slot : slot + 1, :] == row_index).astype(jnp.bfloat16)

    def wait_hidden(source, chunk):
        hidden_copy(source, chunk, 0, across).wait_recv()

    for distance in range(1, n // 2):
        for chunk in range(CHUNKS):
            for sign, onward, here, slot in (
                (-1, has_upper, place_z - distance >= 0, 3 * distance),
                (1, has_lower, place_z + distance <= last_z, 3 * distance + n),
            ):
                source = me + sign * 2 * distance
                pl.when(here)(functools.partial(wait_hidden, source, chunk))
                launch(
                    hidden_copy(source, chunk, slot, me - sign * 2),
                    jnp.logical_and(here, onward),
                )
                launch(hidden_copy(source, chunk, slot + 1, across), here)

    for source in range(n // 2):
        source = 2 * source + lax.rem(across, 2)
        for chunk in range(CHUNKS):
            wait_hidden(source, chunk)

    for step, other in enumerate(others()):
        launch(
            remote(
                meta_out.at[other],
                meta_in.at[me],
                meta_send.at[step],
                meta_recv.at[me],
                peer(other),
            )
        )
    weight_copy.wait()
    own_copy.wait()

    place_index = lax.broadcasted_iota(jnp.int32, (BLOCK, used), 0).astype(jnp.float32)

    def build_dense(source):
        meta = meta_in[source]
        for tile in range(tiles):
            block = jnp.zeros((BLOCK, used), jnp.float32)
            for member in range(4):
                place = meta[member : member + 1, :] - float(tile * BLOCK)
                block = jnp.where(place == place_index, meta[4 + member : 5 + member, :], block)
            dense[source, tile * BLOCK : (tile + 1) * BLOCK, :] = block.astype(jnp.bfloat16)

    def half_rows(which):
        blocks = held[pl.ds(which * half_blocks, half_blocks)]
        return blocks.reshape(tokens, blocks.shape[2])

    for tile in range(tiles):
        cut = slice(tile * BLOCK, (tile + 1) * BLOCK)
        other_half[tile] = jnp.dot(
            half_rows(1 - tok), weight[:, cut], preferred_element_type=jnp.float32
        )
        launch(
            remote(
                other_half.at[tile],
                arrived_half.at[tile],
                half_send.at[tile],
                half_recv.at[tile],
                sibling,
            )
        )
    for tile in range(tiles):
        cut = slice(tile * BLOCK, (tile + 1) * BLOCK)
        own_half[:, cut] = jnp.dot(
            half_rows(tok), weight[:, cut], preferred_element_type=jnp.float32
        )
    for tile in range(tiles):
        cut = slice(tile * BLOCK, (tile + 1) * BLOCK)
        remote(
            other_half.at[tile],
            arrived_half.at[tile],
            half_send.at[tile],
            half_recv.at[tile],
            sibling,
        ).wait_recv()
        own_half[:, cut] = own_half[:, cut] + arrived_half[tile]

    logits = own_half[...]
    peak = jnp.max(logits, axis=1, keepdims=True)
    exponent = jnp.exp(logits - peak)
    mass = jnp.sum(exponent, axis=1, keepdims=True)
    for tile in range(tiles):
        exponents[tile] = exponent[:, tile * BLOCK : (tile + 1) * BLOCK].astype(jnp.bfloat16)

    running = jnp.zeros((tokens, used), jnp.float32)
    for step, other in enumerate(others() + [me]):
        picked = jnp.dot(
            exponents[links_ref[0, other]], onehot[other], preferred_element_type=jnp.float32
        )
        meta = meta_out[other]
        gain = jnp.sum(
            jnp.where(meta[0:4] >= 0.0, meta[4:8], 0.0), axis=0, keepdims=True
        )
        running = running + picked * gain
        if step < n - 1:
            used_out[step] = picked.astype(jnp.bfloat16)
            launch(
                remote(
                    used_out.at[step],
                    used_in.at[me],
                    used_send.at[step],
                    used_recv.at[me],
                    peer(other),
                )
            )
        else:
            used_in[me] = picked.astype(jnp.bfloat16)
    total = jnp.sum(running, axis=1, keepdims=True)

    lane = lax.broadcasted_iota(jnp.int32, (tokens, 128), 1)
    packed = jnp.where(lane == 0, peak, jnp.where(lane == 1, mass, total))
    stats_out[...] = packed.T[0:8, :]
    for step, other in enumerate(others()):
        launch(
            remote(
                stats_out,
                stats_in.at[me],
                stats_send.at[step],
                stats_recv.at[me],
                peer(other),
            )
        )
    stats_in[me] = stats_out[...]

    for other in others():
        remote(
            meta_in.at[other], meta_in.at[other], meta_send.at[0], meta_recv.at[other], sibling
        ).wait_recv()
        build_dense(other)
    build_dense(me)

    for other in others():
        remote(
            stats_out, stats_in.at[other], stats_send.at[0], stats_recv.at[other], sibling
        ).wait_recv()

    peaks = jnp.concatenate([stats_in[v, 0:1, :] for v in range(n)], axis=0)
    masses = jnp.concatenate([stats_in[v, 1:2, :] for v in range(n)], axis=0)
    totals = jnp.concatenate([stats_in[v, 2:3, :] for v in range(n)], axis=0)
    row_peak = jnp.max(peaks, axis=0, keepdims=True)
    shrink = jnp.exp(peaks - row_peak)
    row_mass = jnp.sum(shrink * masses, axis=0, keepdims=True)
    log_ref[...] = row_peak + jnp.log(row_mass)
    share = shrink / row_mass
    row_total = jnp.sum(share * totals, axis=0, keepdims=True)
    factor = float(columns * n) * share / row_total
    factors = jnp.concatenate([factor, jnp.zeros((128 - n, tokens), jnp.float32)], axis=0).T

    for other in others():
        remote(
            used_in.at[other], used_in.at[other], used_send.at[0], used_recv.at[other], sibling
        ).wait_recv()
    for tile in range(tiles):
        cut = slice(tile * BLOCK, (tile + 1) * BLOCK)
        block = jnp.zeros((tokens, BLOCK), jnp.float32)
        for v in range(n):
            piece = lax.dot_general(
                used_in[v],
                dense[v, cut, :],
                (((1,), (1,)), ((), ())),
                preferred_element_type=jnp.float32,
            )
            block = block + factors[:, v : v + 1] * piece
        target_ref[:, cut] = block

    for copy, live in sends:
        if live is None:
            copy.wait_send()
        else:
            pl.when(live)(copy.wait_send)


def fused(hidden_rows, head_weight, block_links, teacher_rows, offsets, link_weights):
    n = lax.axis_size("vocab")
    rows, depth = hidden_rows.shape
    columns = head_weight.shape[1]
    tiles = columns // BLOCK
    tokens = rows * n // 2
    used = teacher_rows.shape[1]
    dma = pltpu.SemaphoreType.DMA
    vmem = pl.BlockSpec(memory_space=pltpu.VMEM)
    log_partition, student_targets = pl.pallas_call(
        functools.partial(fused_kernel, n),
        out_shape=(
            jax.ShapeDtypeStruct((1, tokens), jnp.float32),
            jax.ShapeDtypeStruct((tokens, columns), jnp.float32),
        ),
        in_specs=[pl.BlockSpec(memory_space=pl.ANY)] * 6,
        out_specs=(vmem, vmem),
        scratch_shapes=[
            pltpu.SMEM(block_links.shape, jnp.int32),
            pltpu.VMEM(teacher_rows.shape, jnp.int32),
            pltpu.VMEM(offsets.shape, jnp.int32),
            pltpu.VMEM(link_weights.shape, jnp.bfloat16),
            pltpu.VMEM((n, rows, depth), jnp.bfloat16),
            pltpu.VMEM((depth, columns), jnp.bfloat16),
            pltpu.VMEM((tokens, columns), jnp.float32),
            pltpu.VMEM((tiles, tokens, BLOCK), jnp.float32),
            pltpu.VMEM((tiles, tokens, BLOCK), jnp.float32),
            pltpu.VMEM((tiles, tokens, BLOCK), jnp.bfloat16),
            pltpu.VMEM((n, BLOCK, used), jnp.bfloat16),
            pltpu.VMEM((n, 8, used), jnp.float32),
            pltpu.VMEM((n, 8, used), jnp.float32),
            pltpu.VMEM((n, columns, used), jnp.bfloat16),
            pltpu.VMEM((n - 1, tokens, used), jnp.bfloat16),
            pltpu.VMEM((n, tokens, used), jnp.bfloat16),
            pltpu.VMEM((8, tokens), jnp.float32),
            pltpu.VMEM((n, 8, tokens), jnp.float32),
            dma((6,)),
            dma((3 * n * CHUNKS,)),
            dma((n * CHUNKS,)),
            dma((n - 1,)),
            dma((n,)),
            dma((tiles,)),
            dma((tiles,)),
            dma((n - 1,)),
            dma((n,)),
            dma((n - 1,)),
            dma((n,)),
        ],
        compiler_params=pltpu.CompilerParams(
            collective_id=0, has_side_effects=True, vmem_limit_bytes=60 * 1024 * 1024
        ),
    )(hidden_rows, head_weight, block_links, teacher_rows, offsets, link_weights)
    return log_partition.reshape(tokens), student_targets


def head(hidden_rows, head_weight, block_links, teacher_rows, offsets, link_weights):
    n = lax.axis_size("vocab")
    rows = hidden_rows.shape[0]
    fits = rows % 16 == 0 and rows * n == 256 and n % 2 == 0 and teacher_rows.shape[0] == n
    form = fused if fits and lax.axis_size("tok") == 2 and n <= 16 else local
    return form(hidden_rows, head_weight, block_links, teacher_rows, offsets, link_weights)


def solution(mesh):
    placed = (
        P(("groups", "vocab"), "tok"),
        P("tok", "vocab"),
        P(None, "vocab"),
        P("vocab", None),
        P("vocab", None, None),
        P("vocab", None, None),
    )
    return jax.shard_map(
        head,
        mesh=mesh,
        in_specs=placed,
        out_specs=(P(("groups", "tok")), P(("groups", "tok"), "vocab")),
        check_vma=False,
    )
```

```python
import functools
import math

import jax
import jax.numpy as jnp
from jax import lax
from jax.experimental import pallas as pl
from jax.experimental.pallas import tpu as pltpu
from jax.sharding import PartitionSpec as P

BLOCK = 256
CHUNKS = 2
ORDER = (0, 1, -1, 2, -2, 3, -3)
SB_DEV = 3


def combined_all(value, axis, join):
    pieces = jax.tree.map(lambda part: lax.all_gather(part, axis), value)
    head = jax.tree.map(lambda part: part[0], pieces)
    tail = jax.tree.map(lambda part: part[1:], pieces)
    so_far, _ = lax.scan(lambda so_far, share: (join(so_far, share), None), head, tail)
    return so_far


def dense_blocks(columns, weights, width):
    positions = lax.broadcasted_iota(jnp.int32, (1, 1, width), 2)
    dense_block = jnp.zeros((columns.shape[0], columns.shape[2], width), jnp.bfloat16)
    for member in range(columns.shape[1]):
        dense_block = jnp.where(
            columns[:, member, :, None] == positions, weights[:, member, :, None], dense_block
        )
    return dense_block


def aligned_pieces(picked, columns, weights):
    slot_count = picked.shape[0]
    group_size = math.gcd(slot_count, 16)
    group_count = slot_count // group_size

    def one_group(inputs):
        chosen_in, columns_in, weights_in = inputs
        dense_block = dense_blocks(columns_in, weights_in, BLOCK)
        product = jnp.einsum(
            "gcr,gcd->grd", chosen_in, dense_block, preferred_element_type=jnp.float32
        )
        return product.astype(jnp.bfloat16)

    shaped = (
        picked.reshape((group_count, group_size) + picked.shape[1:]),
        columns.reshape((group_count, group_size) + columns.shape[1:]),
        weights.reshape((group_count, group_size) + weights.shape[1:]),
    )
    return lax.map(one_group, shaped).reshape(slot_count, picked.shape[2], BLOCK)


def collect(received, arrived, blocks_here):
    wanted = lax.broadcasted_iota(jnp.int32, (arrived.shape[0], blocks_here), 1)
    selector = (arrived[:, None] == wanted).astype(jnp.bfloat16)
    summed = jnp.einsum("srd,sj->rjd", received, selector, preferred_element_type=jnp.float32)
    return summed.reshape(received.shape[1], blocks_here * received.shape[2])


def local(hidden_rows, head_weight, block_links, teacher_rows, offsets, link_weights):
    halves = jnp.dot(
        lax.all_gather(hidden_rows, "vocab", axis=0, tiled=True),
        head_weight,
        preferred_element_type=jnp.float32,
    )
    logits = lax.psum_scatter(halves, "tok", scatter_dimension=0, tiled=True)
    local_peak = jnp.max(logits, axis=1)
    local_mass = jnp.sum(jnp.exp(logits - local_peak[:, None]), axis=1)

    def combine(earlier, later):
        top_value = jnp.maximum(earlier[0], later[0])
        joined = earlier[1] * jnp.exp(earlier[0] - top_value) + later[1] * jnp.exp(
            later[0] - top_value
        )
        return (top_value, joined)

    row_peak, row_mass = combined_all((local_peak, local_mass), "vocab", combine)
    exponent = jnp.exp(logits - row_peak[:, None])
    teacher_probs = (exponent / row_mass[:, None]).astype(jnp.bfloat16)
    by_column = teacher_probs.T
    columns_wanted = block_links[0][:, None] * BLOCK + teacher_rows
    picked = jnp.take(by_column, columns_wanted, axis=0)
    targets = block_links[1][:, None]
    pieces = aligned_pieces(picked, offsets, link_weights)
    received, arrived = (
        lax.all_to_all(pieces, "vocab", split_axis=0, concat_axis=0, tiled=True),
        lax.all_to_all(targets, "vocab", split_axis=0, concat_axis=0, tiled=True),
    )
    aligned = collect(received, arrived[:, 0], SB_DEV)
    row_total = lax.psum(jnp.sum(aligned, axis=1), "vocab")
    student_width = aligned.shape[1] * lax.axis_size("vocab")
    student_targets = student_width * aligned / row_total[:, None]
    return (row_peak + jnp.log(row_mass), student_targets)


MESH = pl.DeviceIdType.MESH


def fused_kernel(
    n,
    hidden_ref,
    weight_ref,
    links_hbm,
    rows_hbm,
    offsets_hbm,
    link_weights_hbm,
    log_ref,
    target_ref,
    links_ref,
    rows_ref,
    offsets_ref,
    link_weights_ref,
    held,
    weight,
    own_half,
    other_half,
    arrived_half,
    exponents,
    onehot,
    meta_out,
    meta_in,
    dense,
    used_out,
    used_in,
    stats_out,
    stats_in,
    local_sems,
    hidden_send,
    hidden_recv,
    meta_send,
    meta_recv,
    half_send,
    half_recv,
    used_send,
    used_recv,
    stats_send,
    stats_recv,
):
    group, me, tok = lax.axis_index("groups"), lax.axis_index("vocab"), lax.axis_index("tok")
    columns = weight.shape[1]
    tiles = columns // BLOCK
    half_blocks = n // 2
    tokens = own_half.shape[0]
    used = rows_ref.shape[1]

    def peer(index):
        return (group, index, tok)

    sibling = (group, me, 1 - tok)

    def remote(source, target, send, recv, device):
        return pltpu.make_async_remote_copy(
            src_ref=source,
            dst_ref=target,
            send_sem=send,
            recv_sem=recv,
            device_id=device,
            device_id_type=MESH,
        )

    def others():
        return [lax.rem(me + step, n) for step in range(1, n)]

    across = me + 1 - 2 * lax.rem(me, 2)
    place_z, last_z = me // 2, n // 2 - 1
    has_lower, has_upper = place_z > 0, place_z < last_z

    barrier = pltpu.get_barrier_semaphore()
    for other in (peer(across), sibling):
        pl.semaphore_signal(barrier, inc=1, device_id=other, device_id_type=MESH)

    @pl.when(has_lower)
    def greet_lower():
        pl.semaphore_signal(barrier, inc=1, device_id=peer(me - 2), device_id_type=MESH)

    @pl.when(has_upper)
    def greet_upper():
        pl.semaphore_signal(barrier, inc=1, device_id=peer(me + 2), device_id_type=MESH)

    weight_copy = pltpu.make_async_copy(weight_ref, weight, local_sems.at[0])
    weight_copy.start()
    own_copy = pltpu.make_async_copy(hidden_ref, held.at[me], local_sems.at[1])
    own_copy.start()
    small_copies = [
        pltpu.make_async_copy(source, target, local_sems.at[2 + index])
        for index, (source, target) in enumerate(
            (
                (links_hbm, links_ref),
                (rows_hbm, rows_ref),
                (offsets_hbm, offsets_ref),
                (link_weights_hbm, link_weights_ref),
            )
        )
    ]
    for copy in small_copies:
        copy.start()
    pl.semaphore_wait(barrier, 2 + (has_lower).astype(jnp.int32) + (has_upper).astype(jnp.int32))

    sends = []

    def launch(copy, live=None):
        sends.append((copy, live))
        if live is None:
            copy.start()
        else:
            pl.when(live)(copy.start)

    part = held.shape[1] // CHUNKS

    def held_part(source, chunk):
        return held.at[source, pl.ds(chunk * part, part)]

    def hidden_copy(source, chunk, send, target, own=False):
        here = hidden_ref.at[pl.ds(chunk * part, part)] if own else held_part(source, chunk)
        return remote(
            here,
            held_part(source, chunk),
            hidden_send.at[send * CHUNKS + chunk],
            hidden_recv.at[source * CHUNKS + chunk],
            peer(target),
        )

    for chunk in range(CHUNKS):
        launch(hidden_copy(me, chunk, 1, me - 2, True), has_lower)
        launch(hidden_copy(me, chunk, 2, me + 2, True), has_upper)
        launch(hidden_copy(me, chunk, 0, across, True))

    for copy in small_copies:
        copy.wait()
    values = link_weights_ref[...].astype(jnp.float32)
    for slot in range(n):
        place = offsets_ref[slot] + links_ref[1, slot] * BLOCK
        meta_out[slot, 0:4, :] = place.astype(jnp.float32)
        meta_out[slot, 4:8, :] = values[slot]
    meta_in[me] = meta_out[me]

    row_index = lax.broadcasted_iota(jnp.int32, (BLOCK, used), 0)
    for slot in range(n):
        onehot[slot] = (rows_ref[slot : slot + 1, :] == row_index).astype(jnp.bfloat16)

    def wait_hidden(source, chunk):
        hidden_copy(source, chunk, 0, across).wait_recv()

    for distance in range(1, n // 2):
        for chunk in range(CHUNKS):
            for sign, onward, here, slot in (
                (-1, has_upper, place_z - distance >= 0, 3 * distance),
                (1, has_lower, place_z + distance <= last_z, 3 * distance + n),
            ):
                source = me + sign * 2 * distance
                pl.when(here)(functools.partial(wait_hidden, source, chunk))
                launch(
                    hidden_copy(source, chunk, slot, me - sign * 2),
                    jnp.logical_and(here, onward),
                )
                launch(hidden_copy(source, chunk, slot + 1, across), here)

    for source in range(n // 2):
        source = 2 * source + lax.rem(across, 2)
        for chunk in range(CHUNKS):
            wait_hidden(source, chunk)

    for step, other in enumerate(others()):
        launch(
            remote(
                meta_out.at[other],
                meta_in.at[me],
                meta_send.at[step],
                meta_recv.at[me],
                peer(other),
            )
        )
    weight_copy.wait()
    own_copy.wait()

    place_index = lax.broadcasted_iota(jnp.int32, (BLOCK, used), 0).astype(jnp.float32)

    def build_dense(source):
        meta = meta_in[source]
        for tile in range(tiles):
            block = jnp.zeros((BLOCK, used), jnp.float32)
            for member in range(4):
                place = meta[member : member + 1, :] - float(tile * BLOCK)
                block = jnp.where(place == place_index, meta[4 + member : 5 + member, :], block)
            dense[source, tile * BLOCK : (tile + 1) * BLOCK, :] = block.astype(jnp.bfloat16)

    def half_rows(which):
        blocks = held[pl.ds(which * half_blocks, half_blocks)]
        return blocks.reshape(tokens, blocks.shape[2])

    for tile in range(tiles):
        cut = slice(tile * BLOCK, (tile + 1) * BLOCK)
        other_half[tile] = jnp.dot(
            half_rows(1 - tok), weight[:, cut], preferred_element_type=jnp.float32
        )
        launch(
            remote(
                other_half.at[tile],
                arrived_half.at[tile],
                half_send.at[tile],
                half_recv.at[tile],
                sibling,
            )
        )
    for tile in range(tiles):
        cut = slice(tile * BLOCK, (tile + 1) * BLOCK)
        own_half[:, cut] = jnp.dot(
            half_rows(tok), weight[:, cut], preferred_element_type=jnp.float32
        )
    for tile in range(tiles):
        cut = slice(tile * BLOCK, (tile + 1) * BLOCK)
        remote(
            other_half.at[tile],
            arrived_half.at[tile],
            half_send.at[tile],
            half_recv.at[tile],
            sibling,
        ).wait_recv()
        own_half[:, cut] = own_half[:, cut] + arrived_half[tile]

    logits = own_half[...]
    peak = jnp.max(logits, axis=1, keepdims=True)
    exponent = jnp.exp(logits - peak)
    mass = jnp.sum(exponent, axis=1, keepdims=True)
    for tile in range(tiles):
        exponents[tile] = exponent[:, tile * BLOCK : (tile + 1) * BLOCK].astype(jnp.bfloat16)

    running = jnp.zeros((tokens, used), jnp.float32)
    for step, other in enumerate([lax.rem(me + n // 2 + k, n) for k in ORDER] + [me]):
        picked = jnp.dot(
            exponents[links_ref[0, other]], onehot[other], preferred_element_type=jnp.float32
        )
        meta = meta_out[other]
        gain = jnp.sum(
            jnp.where(meta[0:4] >= 0.0, meta[4:8], 0.0), axis=0, keepdims=True
        )
        running = running + picked * gain
        if step < n - 1:
            used_out[step] = picked.astype(jnp.bfloat16)
            launch(
                remote(
                    used_out.at[step],
                    used_in.at[me],
                    used_send.at[step],
                    used_recv.at[me],
                    peer(other),
                )
            )
        else:
            used_in[me] = picked.astype(jnp.bfloat16)
    total = jnp.sum(running, axis=1, keepdims=True)

    lane = lax.broadcasted_iota(jnp.int32, (tokens, 128), 1)
    packed = jnp.where(lane == 0, peak, jnp.where(lane == 1, mass, total))
    stats_out[...] = packed.T[0:8, :]
    for step, other in enumerate(others()):
        launch(
            remote(
                stats_out,
                stats_in.at[me],
                stats_send.at[step],
                stats_recv.at[me],
                peer(other),
            )
        )
    stats_in[me] = stats_out[...]

    for other in others():
        remote(
            meta_in.at[other], meta_in.at[other], meta_send.at[0], meta_recv.at[other], sibling
        ).wait_recv()
        build_dense(other)
    build_dense(me)

    for other in others():
        remote(
            stats_out, stats_in.at[other], stats_send.at[0], stats_recv.at[other], sibling
        ).wait_recv()

    peaks = jnp.concatenate([stats_in[v, 0:1, :] for v in range(n)], axis=0)
    masses = jnp.concatenate([stats_in[v, 1:2, :] for v in range(n)], axis=0)
    totals = jnp.concatenate([stats_in[v, 2:3, :] for v in range(n)], axis=0)
    row_peak = jnp.max(peaks, axis=0, keepdims=True)
    shrink = jnp.exp(peaks - row_peak)
    row_mass = jnp.sum(shrink * masses, axis=0, keepdims=True)
    log_ref[...] = row_peak + jnp.log(row_mass)
    share = shrink / row_mass
    row_total = jnp.sum(share * totals, axis=0, keepdims=True)
    factor = float(columns * n) * share / row_total
    factors = jnp.concatenate([factor, jnp.zeros((128 - n, tokens), jnp.float32)], axis=0).T

    for other in others():
        remote(
            used_in.at[other], used_in.at[other], used_send.at[0], used_recv.at[other], sibling
        ).wait_recv()
    for tile in range(tiles):
        cut = slice(tile * BLOCK, (tile + 1) * BLOCK)
        block = jnp.zeros((tokens, BLOCK), jnp.float32)
        for v in range(n):
            piece = lax.dot_general(
                used_in[v],
                dense[v, cut, :],
                (((1,), (1,)), ((), ())),
                preferred_element_type=jnp.float32,
            )
            block = block + factors[:, v : v + 1] * piece
        target_ref[:, cut] = block

    for copy, live in sends:
        if live is None:
            copy.wait_send()
        else:
            pl.when(live)(copy.wait_send)


def fused(hidden_rows, head_weight, block_links, teacher_rows, offsets, link_weights):
    n = lax.axis_size("vocab")
    rows, depth = hidden_rows.shape
    columns = head_weight.shape[1]
    tiles = columns // BLOCK
    tokens = rows * n // 2
    used = teacher_rows.shape[1]
    dma = pltpu.SemaphoreType.DMA
    vmem = pl.BlockSpec(memory_space=pltpu.VMEM)
    log_partition, student_targets = pl.pallas_call(
        functools.partial(fused_kernel, n),
        out_shape=(
            jax.ShapeDtypeStruct((1, tokens), jnp.float32),
            jax.ShapeDtypeStruct((tokens, columns), jnp.float32),
        ),
        in_specs=[pl.BlockSpec(memory_space=pl.ANY)] * 6,
        out_specs=(vmem, vmem),
        scratch_shapes=[
            pltpu.SMEM(block_links.shape, jnp.int32),
            pltpu.VMEM(teacher_rows.shape, jnp.int32),
            pltpu.VMEM(offsets.shape, jnp.int32),
            pltpu.VMEM(link_weights.shape, jnp.bfloat16),
            pltpu.VMEM((n, rows, depth), jnp.bfloat16),
            pltpu.VMEM((depth, columns), jnp.bfloat16),
            pltpu.VMEM((tokens, columns), jnp.float32),
            pltpu.VMEM((tiles, tokens, BLOCK), jnp.float32),
            pltpu.VMEM((tiles, tokens, BLOCK), jnp.float32),
            pltpu.VMEM((tiles, tokens, BLOCK), jnp.bfloat16),
            pltpu.VMEM((n, BLOCK, used), jnp.bfloat16),
            pltpu.VMEM((n, 8, used), jnp.float32),
            pltpu.VMEM((n, 8, used), jnp.float32),
            pltpu.VMEM((n, columns, used), jnp.bfloat16),
            pltpu.VMEM((n - 1, tokens, used), jnp.bfloat16),
            pltpu.VMEM((n, tokens, used), jnp.bfloat16),
            pltpu.VMEM((8, tokens), jnp.float32),
            pltpu.VMEM((n, 8, tokens), jnp.float32),
            dma((6,)),
            dma((3 * n * CHUNKS,)),
            dma((n * CHUNKS,)),
            dma((n - 1,)),
            dma((n,)),
            dma((tiles,)),
            dma((tiles,)),
            dma((n - 1,)),
            dma((n,)),
            dma((n - 1,)),
            dma((n,)),
        ],
        compiler_params=pltpu.CompilerParams(
            collective_id=0, has_side_effects=True, vmem_limit_bytes=60 * 1024 * 1024
        ),
    )(hidden_rows, head_weight, block_links, teacher_rows, offsets, link_weights)
    return log_partition.reshape(tokens), student_targets


def head(hidden_rows, head_weight, block_links, teacher_rows, offsets, link_weights):
    n = lax.axis_size("vocab")
    rows = hidden_rows.shape[0]
    fits = rows % 16 == 0 and rows * n == 256 and n % 2 == 0 and teacher_rows.shape[0] == n
    form = fused if fits and lax.axis_size("tok") == 2 and n <= 16 else local
    return form(hidden_rows, head_weight, block_links, teacher_rows, offsets, link_weights)


def solution(mesh):
    placed = (
        P(("groups", "vocab"), "tok"),
        P("tok", "vocab"),
        P(None, "vocab"),
        P("vocab", None),
        P("vocab", None, None),
        P("vocab", None, None),
    )
    return jax.shard_map(
        head,
        mesh=mesh,
        in_specs=placed,
        out_specs=(P(("groups", "tok")), P(("groups", "tok"), "vocab")),
        check_vma=False,
    )
```

```python
import functools
import math

import jax
import jax.numpy as jnp
from jax import lax
from jax.experimental import pallas as pl
from jax.experimental.pallas import tpu as pltpu
from jax.sharding import PartitionSpec as P

BLOCK = 256
CHUNKS = 2
ORDER = (0, 1, -1, 2, -2, 3, -3)
SB_DEV = 3


def combined_all(value, axis, join):
    pieces = jax.tree.map(lambda part: lax.all_gather(part, axis), value)
    head = jax.tree.map(lambda part: part[0], pieces)
    tail = jax.tree.map(lambda part: part[1:], pieces)
    so_far, _ = lax.scan(lambda so_far, share: (join(so_far, share), None), head, tail)
    return so_far


def dense_blocks(columns, weights, width):
    positions = lax.broadcasted_iota(jnp.int32, (1, 1, width), 2)
    dense_block = jnp.zeros((columns.shape[0], columns.shape[2], width), jnp.bfloat16)
    for member in range(columns.shape[1]):
        dense_block = jnp.where(
            columns[:, member, :, None] == positions, weights[:, member, :, None], dense_block
        )
    return dense_block


def aligned_pieces(picked, columns, weights):
    slot_count = picked.shape[0]
    group_size = math.gcd(slot_count, 16)
    group_count = slot_count // group_size

    def one_group(inputs):
        chosen_in, columns_in, weights_in = inputs
        dense_block = dense_blocks(columns_in, weights_in, BLOCK)
        product = jnp.einsum(
            "gcr,gcd->grd", chosen_in, dense_block, preferred_element_type=jnp.float32
        )
        return product.astype(jnp.bfloat16)

    shaped = (
        picked.reshape((group_count, group_size) + picked.shape[1:]),
        columns.reshape((group_count, group_size) + columns.shape[1:]),
        weights.reshape((group_count, group_size) + weights.shape[1:]),
    )
    return lax.map(one_group, shaped).reshape(slot_count, picked.shape[2], BLOCK)


def collect(received, arrived, blocks_here):
    wanted = lax.broadcasted_iota(jnp.int32, (arrived.shape[0], blocks_here), 1)
    selector = (arrived[:, None] == wanted).astype(jnp.bfloat16)
    summed = jnp.einsum("srd,sj->rjd", received, selector, preferred_element_type=jnp.float32)
    return summed.reshape(received.shape[1], blocks_here * received.shape[2])


def local(hidden_rows, head_weight, block_links, teacher_rows, offsets, link_weights):
    halves = jnp.dot(
        lax.all_gather(hidden_rows, "vocab", axis=0, tiled=True),
        head_weight,
        preferred_element_type=jnp.float32,
    )
    logits = lax.psum_scatter(halves, "tok", scatter_dimension=0, tiled=True)
    local_peak = jnp.max(logits, axis=1)
    local_mass = jnp.sum(jnp.exp(logits - local_peak[:, None]), axis=1)

    def combine(earlier, later):
        top_value = jnp.maximum(earlier[0], later[0])
        joined = earlier[1] * jnp.exp(earlier[0] - top_value) + later[1] * jnp.exp(
            later[0] - top_value
        )
        return (top_value, joined)

    row_peak, row_mass = combined_all((local_peak, local_mass), "vocab", combine)
    exponent = jnp.exp(logits - row_peak[:, None])
    teacher_probs = (exponent / row_mass[:, None]).astype(jnp.bfloat16)
    by_column = teacher_probs.T
    columns_wanted = block_links[0][:, None] * BLOCK + teacher_rows
    picked = jnp.take(by_column, columns_wanted, axis=0)
    targets = block_links[1][:, None]
    pieces = aligned_pieces(picked, offsets, link_weights)
    received, arrived = (
        lax.all_to_all(pieces, "vocab", split_axis=0, concat_axis=0, tiled=True),
        lax.all_to_all(targets, "vocab", split_axis=0, concat_axis=0, tiled=True),
    )
    aligned = collect(received, arrived[:, 0], SB_DEV)
    row_total = lax.psum(jnp.sum(aligned, axis=1), "vocab")
    student_width = aligned.shape[1] * lax.axis_size("vocab")
    student_targets = student_width * aligned / row_total[:, None]
    return (row_peak + jnp.log(row_mass), student_targets)


MESH = pl.DeviceIdType.MESH


def fused_kernel(
    n,
    hidden_ref,
    weight_ref,
    links_hbm,
    rows_hbm,
    offsets_hbm,
    link_weights_hbm,
    log_ref,
    target_ref,
    links_ref,
    rows_ref,
    offsets_ref,
    link_weights_ref,
    held,
    weight,
    own_half,
    other_half,
    arrived_half,
    exponents,
    onehot,
    meta_out,
    meta_in,
    dense,
    used_out,
    used_in,
    stats_out,
    stats_in,
    local_sems,
    hidden_send,
    hidden_recv,
    meta_send,
    meta_recv,
    half_send,
    half_recv,
    used_send,
    used_recv,
    stats_send,
    stats_recv,
):
    group, me, tok = lax.axis_index("groups"), lax.axis_index("vocab"), lax.axis_index("tok")
    columns = weight.shape[1]
    tiles = columns // BLOCK
    half_blocks = n // 2
    tokens = own_half.shape[0]
    used = rows_ref.shape[1]

    def peer(index):
        return (group, index, tok)

    sibling = (group, me, 1 - tok)

    def remote(source, target, send, recv, device):
        return pltpu.make_async_remote_copy(
            src_ref=source,
            dst_ref=target,
            send_sem=send,
            recv_sem=recv,
            device_id=device,
            device_id_type=MESH,
        )

    def others():
        return [lax.rem(me + step, n) for step in range(1, n)]

    across = me + 1 - 2 * lax.rem(me, 2)
    place_z, last_z = me // 2, n // 2 - 1
    has_lower, has_upper = place_z > 0, place_z < last_z

    barrier = pltpu.get_barrier_semaphore()
    for other in (peer(across), sibling):
        pl.semaphore_signal(barrier, inc=1, device_id=other, device_id_type=MESH)

    @pl.when(has_lower)
    def greet_lower():
        pl.semaphore_signal(barrier, inc=1, device_id=peer(me - 2), device_id_type=MESH)

    @pl.when(has_upper)
    def greet_upper():
        pl.semaphore_signal(barrier, inc=1, device_id=peer(me + 2), device_id_type=MESH)

    weight_copy = pltpu.make_async_copy(weight_ref, weight, local_sems.at[0])
    weight_copy.start()
    own_copy = pltpu.make_async_copy(hidden_ref, held.at[me], local_sems.at[1])
    own_copy.start()
    small_copies = [
        pltpu.make_async_copy(source, target, local_sems.at[2 + index])
        for index, (source, target) in enumerate(
            (
                (links_hbm, links_ref),
                (rows_hbm, rows_ref),
                (offsets_hbm, offsets_ref),
                (link_weights_hbm, link_weights_ref),
            )
        )
    ]
    for copy in small_copies:
        copy.start()
    pl.semaphore_wait(barrier, 2 + (has_lower).astype(jnp.int32) + (has_upper).astype(jnp.int32))

    sends = []

    def launch(copy, live=None):
        sends.append((copy, live))
        if live is None:
            copy.start()
        else:
            pl.when(live)(copy.start)

    part = held.shape[1] // CHUNKS

    def held_part(source, chunk):
        return held.at[source, pl.ds(chunk * part, part)]

    def hidden_copy(source, chunk, send, target, own=False):
        here = hidden_ref.at[pl.ds(chunk * part, part)] if own else held_part(source, chunk)
        return remote(
            here,
            held_part(source, chunk),
            hidden_send.at[send * CHUNKS + chunk],
            hidden_recv.at[source * CHUNKS + chunk],
            peer(target),
        )

    for chunk in range(CHUNKS):
        launch(hidden_copy(me, chunk, 1, me - 2, True), has_lower)
        launch(hidden_copy(me, chunk, 2, me + 2, True), has_upper)
        launch(hidden_copy(me, chunk, 0, across, True))

    for copy in small_copies:
        copy.wait()
    values = link_weights_ref[...].astype(jnp.float32)
    for slot in range(n):
        place = offsets_ref[slot] + links_ref[1, slot] * BLOCK
        meta_out[slot, 0:4, :] = place.astype(jnp.float32)
        meta_out[slot, 4:8, :] = values[slot]
    meta_in[me] = meta_out[me]

    row_index = lax.broadcasted_iota(jnp.int32, (BLOCK, used), 0)
    for slot in range(n):
        onehot[slot] = (rows_ref[slot : slot + 1, :] == row_index).astype(jnp.bfloat16)

    def wait_hidden(source, chunk):
        hidden_copy(source, chunk, 0, across).wait_recv()

    for distance in range(1, n // 2):
        for chunk in range(CHUNKS):
            for sign, onward, here, slot in (
                (-1, has_upper, place_z - distance >= 0, 3 * distance),
                (1, has_lower, place_z + distance <= last_z, 3 * distance + n),
            ):
                source = me + sign * 2 * distance
                pl.when(here)(functools.partial(wait_hidden, source, chunk))
                launch(
                    hidden_copy(source, chunk, slot, me - sign * 2),
                    jnp.logical_and(here, onward),
                )
                launch(hidden_copy(source, chunk, slot + 1, across), here)

    for source in range(n // 2):
        source = 2 * source + lax.rem(across, 2)
        for chunk in range(CHUNKS):
            wait_hidden(source, chunk)

    weight_copy.wait()
    own_copy.wait()

    place_index = lax.broadcasted_iota(jnp.int32, (BLOCK, used), 0).astype(jnp.float32)

    def build_dense(source):
        meta = meta_in[source]
        for tile in range(tiles):
            block = jnp.zeros((BLOCK, used), jnp.float32)
            for member in range(4):
                place = meta[member : member + 1, :] - float(tile * BLOCK)
                block = jnp.where(place == place_index, meta[4 + member : 5 + member, :], block)
            dense[source, tile * BLOCK : (tile + 1) * BLOCK, :] = block.astype(jnp.bfloat16)

    def half_rows(which):
        blocks = held[pl.ds(which * half_blocks, half_blocks)]
        return blocks.reshape(tokens, blocks.shape[2])

    for tile in range(tiles):
        cut = slice(tile * BLOCK, (tile + 1) * BLOCK)
        other_half[tile] = jnp.dot(
            half_rows(1 - tok), weight[:, cut], preferred_element_type=jnp.float32
        )
        launch(
            remote(
                other_half.at[tile],
                arrived_half.at[tile],
                half_send.at[tile],
                half_recv.at[tile],
                sibling,
            )
        )
    for tile in range(tiles):
        cut = slice(tile * BLOCK, (tile + 1) * BLOCK)
        own_half[:, cut] = jnp.dot(
            half_rows(tok), weight[:, cut], preferred_element_type=jnp.float32
        )
    for step, other in enumerate(others()):
        launch(
            remote(
                meta_out.at[other],
                meta_in.at[me],
                meta_send.at[step],
                meta_recv.at[me],
                peer(other),
            )
        )
    for tile in range(tiles):
        cut = slice(tile * BLOCK, (tile + 1) * BLOCK)
        remote(
            other_half.at[tile],
            arrived_half.at[tile],
            half_send.at[tile],
            half_recv.at[tile],
            sibling,
        ).wait_recv()
        own_half[:, cut] = own_half[:, cut] + arrived_half[tile]

    logits = own_half[...]
    peak = jnp.max(logits, axis=1, keepdims=True)
    exponent = jnp.exp(logits - peak)
    mass = jnp.sum(exponent, axis=1, keepdims=True)
    for tile in range(tiles):
        exponents[tile] = exponent[:, tile * BLOCK : (tile + 1) * BLOCK].astype(jnp.bfloat16)

    running = jnp.zeros((tokens, used), jnp.float32)
    for step, other in enumerate([lax.rem(me + n // 2 + k, n) for k in ORDER] + [me]):
        picked = jnp.dot(
            exponents[links_ref[0, other]], onehot[other], preferred_element_type=jnp.float32
        )
        meta = meta_out[other]
        gain = jnp.sum(
            jnp.where(meta[0:4] >= 0.0, meta[4:8], 0.0), axis=0, keepdims=True
        )
        running = running + picked * gain
        if step < n - 1:
            used_out[step] = picked.astype(jnp.bfloat16)
            launch(
                remote(
                    used_out.at[step],
                    used_in.at[me],
                    used_send.at[step],
                    used_recv.at[me],
                    peer(other),
                )
            )
        else:
            used_in[me] = picked.astype(jnp.bfloat16)
    total = jnp.sum(running, axis=1, keepdims=True)

    lane = lax.broadcasted_iota(jnp.int32, (tokens, 128), 1)
    packed = jnp.where(lane == 0, peak, jnp.where(lane == 1, mass, total))
    stats_out[...] = packed.T[0:8, :]
    for step, other in enumerate(others()):
        launch(
            remote(
                stats_out,
                stats_in.at[me],
                stats_send.at[step],
                stats_recv.at[me],
                peer(other),
            )
        )
    stats_in[me] = stats_out[...]

    for other in others():
        remote(
            meta_in.at[other], meta_in.at[other], meta_send.at[0], meta_recv.at[other], sibling
        ).wait_recv()
        build_dense(other)
    build_dense(me)

    for other in others():
        remote(
            stats_out, stats_in.at[other], stats_send.at[0], stats_recv.at[other], sibling
        ).wait_recv()

    peaks = jnp.concatenate([stats_in[v, 0:1, :] for v in range(n)], axis=0)
    masses = jnp.concatenate([stats_in[v, 1:2, :] for v in range(n)], axis=0)
    totals = jnp.concatenate([stats_in[v, 2:3, :] for v in range(n)], axis=0)
    row_peak = jnp.max(peaks, axis=0, keepdims=True)
    shrink = jnp.exp(peaks - row_peak)
    row_mass = jnp.sum(shrink * masses, axis=0, keepdims=True)
    log_ref[...] = row_peak + jnp.log(row_mass)
    share = shrink / row_mass
    row_total = jnp.sum(share * totals, axis=0, keepdims=True)
    factor = float(columns * n) * share / row_total
    factors = jnp.concatenate([factor, jnp.zeros((128 - n, tokens), jnp.float32)], axis=0).T

    for other in others():
        remote(
            used_in.at[other], used_in.at[other], used_send.at[0], used_recv.at[other], sibling
        ).wait_recv()
    for tile in range(tiles):
        cut = slice(tile * BLOCK, (tile + 1) * BLOCK)
        block = jnp.zeros((tokens, BLOCK), jnp.float32)
        for v in range(n):
            piece = lax.dot_general(
                used_in[v],
                dense[v, cut, :],
                (((1,), (1,)), ((), ())),
                preferred_element_type=jnp.float32,
            )
            block = block + factors[:, v : v + 1] * piece
        target_ref[:, cut] = block

    for copy, live in sends:
        if live is None:
            copy.wait_send()
        else:
            pl.when(live)(copy.wait_send)


def fused(hidden_rows, head_weight, block_links, teacher_rows, offsets, link_weights):
    n = lax.axis_size("vocab")
    rows, depth = hidden_rows.shape
    columns = head_weight.shape[1]
    tiles = columns // BLOCK
    tokens = rows * n // 2
    used = teacher_rows.shape[1]
    dma = pltpu.SemaphoreType.DMA
    vmem = pl.BlockSpec(memory_space=pltpu.VMEM)
    log_partition, student_targets = pl.pallas_call(
        functools.partial(fused_kernel, n),
        out_shape=(
            jax.ShapeDtypeStruct((1, tokens), jnp.float32),
            jax.ShapeDtypeStruct((tokens, columns), jnp.float32),
        ),
        in_specs=[pl.BlockSpec(memory_space=pl.ANY)] * 6,
        out_specs=(vmem, vmem),
        scratch_shapes=[
            pltpu.SMEM(block_links.shape, jnp.int32),
            pltpu.VMEM(teacher_rows.shape, jnp.int32),
            pltpu.VMEM(offsets.shape, jnp.int32),
            pltpu.VMEM(link_weights.shape, jnp.bfloat16),
            pltpu.VMEM((n, rows, depth), jnp.bfloat16),
            pltpu.VMEM((depth, columns), jnp.bfloat16),
            pltpu.VMEM((tokens, columns), jnp.float32),
            pltpu.VMEM((tiles, tokens, BLOCK), jnp.float32),
            pltpu.VMEM((tiles, tokens, BLOCK), jnp.float32),
            pltpu.VMEM((tiles, tokens, BLOCK), jnp.bfloat16),
            pltpu.VMEM((n, BLOCK, used), jnp.bfloat16),
            pltpu.VMEM((n, 8, used), jnp.float32),
            pltpu.VMEM((n, 8, used), jnp.float32),
            pltpu.VMEM((n, columns, used), jnp.bfloat16),
            pltpu.VMEM((n - 1, tokens, used), jnp.bfloat16),
            pltpu.VMEM((n, tokens, used), jnp.bfloat16),
            pltpu.VMEM((8, tokens), jnp.float32),
            pltpu.VMEM((n, 8, tokens), jnp.float32),
            dma((6,)),
            dma((3 * n * CHUNKS,)),
            dma((n * CHUNKS,)),
            dma((n - 1,)),
            dma((n,)),
            dma((tiles,)),
            dma((tiles,)),
            dma((n - 1,)),
            dma((n,)),
            dma((n - 1,)),
            dma((n,)),
        ],
        compiler_params=pltpu.CompilerParams(
            collective_id=0, has_side_effects=True, vmem_limit_bytes=60 * 1024 * 1024
        ),
    )(hidden_rows, head_weight, block_links, teacher_rows, offsets, link_weights)
    return log_partition.reshape(tokens), student_targets


def head(hidden_rows, head_weight, block_links, teacher_rows, offsets, link_weights):
    n = lax.axis_size("vocab")
    rows = hidden_rows.shape[0]
    fits = rows % 16 == 0 and rows * n == 256 and n % 2 == 0 and teacher_rows.shape[0] == n
    form = fused if fits and lax.axis_size("tok") == 2 and n <= 16 else local
    return form(hidden_rows, head_weight, block_links, teacher_rows, offsets, link_weights)


def solution(mesh):
    placed = (
        P(("groups", "vocab"), "tok"),
        P("tok", "vocab"),
        P(None, "vocab"),
        P("vocab", None),
        P("vocab", None, None),
        P("vocab", None, None),
    )
    return jax.shard_map(
        head,
        mesh=mesh,
        in_specs=placed,
        out_specs=(P(("groups", "tok")), P(("groups", "tok"), "vocab")),
        check_vma=False,
    )
```
